256 devices in a mesh: rep: 4 (over y_lo, core), fsdp: 64 (over x, z, y_hi).
Axes of the slice: x: 4, y: 4 (y_hi: 2, y_lo: 2; y = y_hi * 2 + y_lo), z: 8, core: 2. Of those that a mesh axis runs over, the one named last changes fastest.
Arguments:
- tokens: bfloat16 [4, 16384, 8192], P('rep', 'fsdp'), may hold values from -16 to 16
- weight: bfloat16 [4, 8192, 512], P('rep', 'fsdp'), may hold values from -6 to 6
- moment: bfloat16 [4, 8192, 512], P('rep', 'fsdp'), may hold values from -6 to 6
- second: bfloat16 [4, 8192, 512], P('rep', 'fsdp'), may hold values from 0.049804688 to 2
- cotangent: bfloat16 [4, 16384, 512], P('rep', 'fsdp'), may hold values from -12 to 12
- lengths: int32 [4, 4], P('rep'), may hold values from 2048 to 4096
- fragment: int32 [4], replicated, may hold values from 0 to 3, each once
- anchor: float32 [8192, 512], P('fsdp'), may hold values from -6 to 6
- velocity: float32 [8192, 512], P('fsdp'), may hold values from -4 to 4
- outer_grad: bfloat16 [4, 8192, 128], P('rep', 'fsdp'), may hold values from -4 to 4
Outputs:
- projected: bfloat16 [4, 16384, 512], P('rep', 'fsdp')
- input_grad: bfloat16 [4, 16384, 8192], P('rep', 'fsdp')
- weight_new: bfloat16 [4, 8192, 512], P('rep', 'fsdp')
- moment_new: bfloat16 [4, 8192, 512], P('rep', 'fsdp')
- second_new: bfloat16 [4, 8192, 512], P('rep', 'fsdp')
- anchor_new: float32 [8192, 128], P('fsdp')
- velocity_new: float32 [8192, 128], P('fsdp')
- drift: float32 [4, 8192, 512], P('rep', 'fsdp')
The draws below stay inside these ranges and needn't reach their ends.
Inputs may be any that keep to these rules, and one draw needn't show every extreme that they name: fragment names each fragment index once.
All inputs are finite; a program needn't handle non-finite values.
Results may differ from the reference program's by a relative error of at most 0.0059.
Values may be sent and summed in bfloat16 or wider, within the bound.
No kernel may reach another device: no remote copies, remote signals or barrier semaphores. Data moves between devices by JAX's collectives and lax.ppermute only.
A program may use at most 128 MiB of HBM per device.

```python
import math
import jax
import jax.numpy as jnp
from jax import lax

D = 8192
HEAD = 128
KV_HEADS = 4
KV = 512
TOKENS = 16384
SEQ_LEN = 4096
SEQS = 4
REPS = 4


def place_ends(entries, key, smallest, high):
    longest = entries.shape.index(max(entries.shape))
    spots = []
    for shift in (0, 1):
        where = [jax.random.randint(jax.random.fold_in(key, axis), (), 0, length) for axis, length in enumerate(entries.shape)]
        where[longest] = (where[longest] + shift) % entries.shape[longest]
        spots.append(tuple(where))
    return entries.at[spots[0]].set(smallest).at[spots[1]].set(high)


def with_spikes(entries, stream_key, source, target, blocks, factor):
    owner, partner = [(jnp.arange(entries.shape[dim]) // (entries.shape[dim] // blocks)).reshape([-1 if axis == dim else 1 for axis in range(entries.ndim)]) for dim in (source, target)]
    chosen = jax.random.permutation(stream_key, blocks)[partner]
    strong = (owner == chosen) | (owner == (partner + blocks // 2) % blocks)
    return jnp.where(strong, factor * entries, entries)


def block_scale(rng, shape, pieces, least, high):
    level = 1.0
    for position, parts in pieces:
        draws = jax.random.uniform(jax.random.fold_in(jax.random.fold_in(rng, 6), position), (parts,), jnp.float32, least / len(pieces), high / len(pieces))
        level = level * jnp.repeat(jnp.exp(draws), shape[position] // parts).reshape((-1,) + (1,) * (len(shape) - 1 - position))
    return level


def normal_values(own_key, extent, scale, reach, pieces=(), held_as=jnp.bfloat16):
    level = block_scale(own_key, extent, pieces, -0.22, 0.18) if pieces else 1.0
    values = jax.random.normal(own_key, extent, jnp.float32) * scale * level
    return jnp.minimum(jnp.maximum(values, -reach), reach).astype(held_as)


def bell_draw_with(key, dims, width, limit, cuts, heavy, kind=jnp.bfloat16):
    array = width * jax.random.normal(key, dims, jnp.float32)
    if cuts:
        array = array * block_scale(key, dims, cuts, -0.22, 0.18)
    return jnp.clip(with_spikes(array, jax.random.fold_in(key, 3), *heavy), -limit, limit).astype(kind)


def setup_inputs(seed: int = 0) -> dict:
    arg_keys = jax.random.split(jax.random.key(seed), 11)
    return {
        "tokens": bell_draw_with(arg_keys[0], (REPS, TOKENS, D), 1.0, 16.0, ((0, 4), (1, 64)), (1, 2, 64, 4.0)),
        "weight": normal_values(arg_keys[1], (REPS, D, KV), 1.0, 6.0, ((0, 4), (1, 64))),
        "moment": normal_values(arg_keys[2], (REPS, D, KV), 0.5, 6.0, ((0, 4), (1, 64))),
        "second": jnp.clip(jnp.exp(math.log(2.0) - 3.6927934 * jax.random.uniform(arg_keys[3], (REPS, D, KV), jnp.float32) ** block_scale(arg_keys[3], (REPS, D, KV), ((0, 4), (1, 64)), -0.2, 0.2)), 0.049804688, 2.0).astype(jnp.bfloat16),
        "cotangent": normal_values(arg_keys[4], (REPS, TOKENS, KV), 2.0, 12.0, ((0, 4), (1, 64))),
        "lengths": place_ends(jax.random.randint(arg_keys[5], (REPS, SEQS), SEQ_LEN // 2, SEQ_LEN + 1), jax.random.fold_in(arg_keys[5], 1), SEQ_LEN // 2, SEQ_LEN).astype(jnp.int32),
        "fragment": jax.random.permutation(arg_keys[6], KV_HEADS).astype(jnp.int32),
        "anchor": normal_values(arg_keys[7], (D, KV), 1.0, 6.0, ((0, 64),), jnp.float32),
        "velocity": normal_values(arg_keys[8], (D, KV), 0.3, 4.0, ((0, 64),), jnp.float32),
        "outer_grad": normal_values(arg_keys[9], (REPS, D, HEAD), 0.3, 4.0, ((0, 4), (1, 64))),
    }


def reference(tokens, weight, moment, second, cotangent, lengths, fragment, anchor, velocity, outer_grad):
    scale = 1.0 / math.sqrt(D)
    positions = jnp.arange(TOKENS, dtype=jnp.int32)
    sequence = positions // SEQ_LEN
    offset = positions % SEQ_LEN
    frag = fragment[0].astype(jnp.int32)
    start = (frag * HEAD).astype(jnp.int32)
    outer_mean = lax.optimization_barrier(jnp.sum(outer_grad.astype(jnp.float32), axis=0)) / REPS
    vel_cols = lax.dynamic_slice_in_dim(velocity, start, HEAD, 1)
    anc_cols = lax.dynamic_slice_in_dim(anchor, start, HEAD, 1)
    velocity_new = 0.9 * vel_cols + outer_mean
    anchor_new = anc_cols - 0.7 * (outer_mean + 0.9 * velocity_new)
    proj_list, igrad_list, weight_list, mom_list, sec_list, drift_list = ([], [], [], [], [], [])
    for replica in range(REPS):
        live = (offset < lengths[replica][sequence]).astype(jnp.float32)
        proj = jnp.dot(tokens[replica], weight[replica], preferred_element_type=jnp.float32) * scale
        proj_list.append(proj.astype(jnp.bfloat16))
        masked = (cotangent[replica].astype(jnp.float32) * live[:, None]).astype(jnp.bfloat16)
        grad = jnp.dot(tokens[replica].T, masked, preferred_element_type=jnp.float32) * scale
        igrad = jnp.dot(masked, weight[replica].T, preferred_element_type=jnp.float32) * scale
        igrad_list.append(igrad.astype(jnp.bfloat16))
        first = 0.9 * moment[replica].astype(jnp.float32) + 0.1 * grad
        sec = 0.95 * second[replica].astype(jnp.float32) + 0.05 * grad * grad
        mom_list.append(first.astype(jnp.bfloat16))
        sec_list.append(sec.astype(jnp.bfloat16))
        old = weight[replica].astype(jnp.float32)
        stepped = old - 0.01 * (first / (jnp.sqrt(sec) + 1e-08) + 0.1 * old)
        blocks = []
        for order in range(KV_HEADS):
            begin = (fragment[order] * HEAD).astype(jnp.int32)
            blocks.append(lax.dynamic_slice_in_dim(anchor, begin, HEAD, 1) - lax.dynamic_slice_in_dim(stepped, begin, HEAD, 1))
        drift_list.append(jnp.concatenate(blocks, axis=1))
        mixed = 0.5 * lax.dynamic_slice_in_dim(stepped, start, HEAD, 1) + 0.5 * anchor_new
        stepped = lax.dynamic_update_slice_in_dim(stepped, mixed, start, 1)
        weight_list.append(stepped.astype(jnp.bfloat16))
    return (jnp.stack(proj_list), jnp.stack(igrad_list), jnp.stack(weight_list), jnp.stack(mom_list), jnp.stack(sec_list), anchor_new, velocity_new, jnp.stack(drift_list))
```

```python
import functools
import math

import jax
import jax.numpy as jnp
from jax import lax
from jax.experimental import pallas as pl
from jax.experimental.pallas import tpu as pltpu
from jax.sharding import PartitionSpec as P

D = 8192
KV = 512
HEAD = 128
NX, NZ, NY = 4, 8, 2
SLOT = D // (NX * NZ)
ROWS = SLOT // NY
PART = KV // 2
LOAD = 3 * D // (2 * NZ)
SCALE = 1.0 / math.sqrt(D)
AXES = ("rep", "fsdp")
BF = jnp.bfloat16
F32 = jnp.float32


def device_index(x, z, y, core):
    y_hi, y_lo = y // 2, y % 2
    return (y_lo * 2 + core) * 64 + (x * NZ + z) * NY + y_hi


def moved(value, dx=0, dz=0, dy=0, dcore=0):
    pairs = []
    for x in range(NX):
        for z in range(NZ):
            for y in range(4):
                for core in range(2):
                    source = device_index(x, z, y, core)
                    target = device_index(
                        (x + dx) % NX, (z + dz) % NZ, (y + dy) % 4, (core + dcore) % 2
                    )
                    pairs.append((source, target))
    return lax.ppermute(value, AXES, sorted(pairs))


def swap_y_lo(value):
    pairs = []
    for rep in range(4):
        for place in range(64):
            pairs.append((rep * 64 + place, (rep ^ 2) * 64 + place))
    return lax.ppermute(value, AXES, pairs)


def together(*values):
    return lax.optimization_barrier(values)


def both_ways(to_right, to_left, axis):
    to_right, to_left = together(to_right, to_left)
    return together(moved(to_right, **{axis: 1}), moved(to_left, **{axis: -1}))


def contract(left, right, left_dim, right_dim):
    return lax.dot_general(
        left, right, (((left_dim,), (right_dim,)), ((), ())), preferred_element_type=F32
    )


def call(
    kernel, grid, scalars, ins, outs, flops, moved_bytes, scratch=(), aliases=None, limit=20
):
    shapes = [jax.ShapeDtypeStruct(shape, kind) for shape, kind, _ in outs]
    return pl.pallas_call(
        kernel,
        out_shape=shapes,
        grid_spec=pltpu.PrefetchScalarGridSpec(
            num_scalar_prefetch=1,
            grid=grid,
            in_specs=[spec for _, spec in ins],
            out_specs=[spec for _, _, spec in outs],
            scratch_shapes=list(scratch),
        ),
        input_output_aliases=aliases or {},
        compiler_params=pltpu.CompilerParams(vmem_limit_bytes=limit << 20),
        cost_estimate=pl.CostEstimate(
            flops=flops, bytes_accessed=moved_bytes, transcendentals=0
        ),
    )(scalars, *[value for value, _ in ins])


def whole(*shape):
    return pl.BlockSpec(shape, lambda *_: (0,) * len(shape))


def live_rows(cotangent, at):
    row = lax.broadcasted_iota(jnp.int32, cotangent.shape, 0)
    return jnp.where(row < at[3], cotangent, jnp.zeros_like(cotangent))


def token_specs(count, shift, y=None):
    def spec(col):
        if y is None:
            return pl.BlockSpec((count, SLOT), lambda i, at: (0, col * NZ + lax.rem(at[1] + shift, NZ)))

        def place(i, at):
            z = lax.rem(at[1] + (shift(i) if callable(shift) else shift), NZ)
            return 0, (col * NZ + z) * NY + (at[2] if y == 0 else 1 - at[2])

        return pl.BlockSpec((count, ROWS), place)

    return [spec(col) for col in range(NX)]


def joined(refs):
    return jnp.concatenate([ref[...] for ref in refs], axis=1)


def first_kernel(at, *refs):
    toks, (cotangent, rows, out) = refs[:NX], refs[NX:]
    rows[...] = live_rows(cotangent[...], at).T
    out[0] = contract(rows[PART:], joined(toks), 1, 0).astype(BF)


def first_block(tokens, cotangent, at):
    count = tokens.shape[0]
    ins = [(tokens, spec) for spec in token_specs(count, lambda i: NZ // 2, 1)]
    ins += [(cotangent, whole(count, KV))]
    outs = [((KV, count), BF, whole(KV, count))]
    outs += [((1, PART, NX * ROWS), BF, whole(1, PART, NX * ROWS))]
    return call(first_kernel, (1,), at, ins, outs, PART * count * NX * SLOT, 1 << 20)


def twin_kernel(at, *refs):
    toks, rows, out = refs[:NX], *refs[NX:]
    out[0] = contract(rows[...], joined(toks), 1, 0).astype(BF)


def twin_blocks(tokens, rows, at, steps):
    count = tokens.shape[0]

    def shift(i):
        value = steps[-1] % NZ
        for order in range(len(steps) - 2, -1, -1):
            value = jnp.where(i == order, steps[order] % NZ, value)
        return value

    ins = [(tokens, spec) for spec in token_specs(count, shift, 1)] + [(rows, whole(PART, count))]
    block = pl.BlockSpec((1, PART, NX * ROWS), lambda i, at: (i, 0, 0))
    outs = [((len(steps), PART, NX * ROWS), BF, block)]
    flops = 2 * PART * count * NX * ROWS * len(steps)
    return call(twin_kernel, (len(steps),), at, ins, outs, flops, len(steps) << 19)[0]


def terms(toks, rows, y_hi):
    wide = [contract(rows[:PART], tok[...], 1, 0) for tok in toks]
    begin = pl.multiple_of(y_hi * ROWS, ROWS)
    narrow = jnp.concatenate([tok[:, pl.ds(begin, ROWS)] for tok in toks], axis=1)
    return wide + [contract(rows[PART:], narrow, 1, 0)]


def far_kernel(at, *refs):
    toks, (rows, came, out_r, out_l) = refs[:NX], refs[NX:]
    parts = terms(toks, rows, at[2])
    parts[NX] = parts[NX] + came[0].astype(F32)
    value = jnp.concatenate(parts, axis=1).astype(BF)
    out_r[...] = value[: PART // 2]
    out_l[...] = value[PART // 2 :]


def far_block(tokens, rows, came, at):
    count = tokens.shape[0]
    ins = [(tokens, spec) for spec in token_specs(count, 4)]
    ins += [(rows, whole(KV, count)), (came, whole(1, PART, NX * ROWS))]
    outs = [((PART // 2, LOAD), BF, whole(PART // 2, LOAD))] * 2
    return call(far_kernel, (1,), at, ins, outs, 2 * PART * count * LOAD, 3 << 19)


def step_kernel(upper, at, *refs):
    toks, (rows, came, moving, out) = refs[:NX], refs[NX:]
    parts = terms(toks, rows, at[2])
    parts[NX] = parts[NX] + came[0].astype(F32)
    size = moving.shape[0]
    begin = PART - size if upper else 0
    col = 0
    for part in parts:
        cols = slice(col, col + part.shape[1])
        col += part.shape[1]
        rows_in = slice(begin, begin + size)
        out[rows_in, cols] = (part[rows_in] + moving[:, cols].astype(F32)).astype(BF)
        if size < PART:
            rest = slice(0, begin) if upper else slice(size, PART)
            out[rest, cols] = part[rest].astype(BF)


def step_block(tokens, rows, came, order, moving, at, step):
    count = tokens.shape[0]
    ins = [(tokens, spec) for spec in token_specs(count, step % NZ)]
    ins += [
        (rows, whole(KV, count)),
        (came, pl.BlockSpec((1, PART, NX * ROWS), lambda i, at: (order, 0, 0))),
        (moving, whole(*moving.shape)),
    ]
    outs = [((PART, LOAD), BF, whole(PART, LOAD))]
    kernel = functools.partial(step_kernel, step < 0)
    return call(kernel, (1,), at, ins, outs, 2 * PART * count * LOAD, 5 << 19)[0]


def last_kernel(at, tok, rows, came, *refs):
    moving_p, moving_q, (own, out_1, out_2, out_3) = refs[:2], refs[2:4], refs[4:]
    i = pl.program_id(0)
    wide, narrow = terms([tok], rows, at[2])
    wide = wide + (moving_p[0][...].astype(F32) + moving_p[1][...].astype(F32))
    narrow = narrow + came[0].astype(F32)
    narrow = narrow + (moving_q[0][...].astype(F32) + moving_q[1][...].astype(F32))
    for step, out in ((0, own), (1, out_1), (2, out_2), (3, out_3)):

        @pl.when(i == step)
        def _(out=out):
            out[:, :SLOT] = wide.astype(out.dtype)
            out[:, SLOT:] = narrow.astype(out.dtype)


def last_block(tokens, rows, came, order, right, left, at):
    count = tokens.shape[0]

    def column(i, at):
        return lax.rem(at[0] + i, NX)

    tok = pl.BlockSpec((count, SLOT), lambda i, at: (0, column(i, at) * NZ + at[1]))
    wide = pl.BlockSpec((PART, SLOT), lambda i, at: (0, column(i, at)))
    narrow = pl.BlockSpec((PART, ROWS), lambda i, at: (0, NX * NY + column(i, at)))
    twin = pl.BlockSpec((1, PART, ROWS), lambda i, at: (order, 0, column(i, at)))
    ins = [(tokens, tok), (rows, whole(KV, count)), (came, twin)]
    ins += [(right, wide), (left, wide), (right, narrow), (left, narrow)]
    size = SLOT + ROWS
    outs = [((PART, size), F32, whole(PART, size))]
    outs += [((PART, size), BF, whole(PART, size))] * 3
    return call(last_kernel, (NX,), at, ins, outs, 2 * PART * count * LOAD, 4 << 20)


def split_kernel(at, own, in_1, in_2, in_3, keep, send):
    value = own[...] + (
        in_1[...].astype(F32) + in_2[...].astype(F32) + in_3[...].astype(F32)
    )
    keep[PART:] = value[:, SLOT:]
    for y in range(NY):

        @pl.when(at[2] == y)
        def _(y=y):
            keep[:PART] = value[:, y * ROWS : (y + 1) * ROWS]
            send[...] = value[:, (1 - y) * ROWS : (2 - y) * ROWS].astype(BF)


def split_y(own, came, at):
    full = whole(PART, SLOT + ROWS)
    ins = [(own, full)] + [(value, full) for value in came]
    outs = [((KV, ROWS), F32, whole(KV, ROWS)), ((PART, ROWS), BF, whole(PART, ROWS))]
    return call(split_kernel, (1,), at, ins, outs, 1 << 20, 3 << 19)


def spread_x(pieces):
    pieces = together(*pieces)
    return together(*[moved(value, dx=step) for step, value in zip((1, 2, 3), pieces)])


def weight_kernel(first, last, at, tok, cotangent, near, twin, *rest):
    sums, (out, grad, both) = (None if first else rest[0]), rest[-3:]
    z, y_hi = at[1], at[2]
    for order in range(NZ):
        slot = lax.rem(z + order, NZ) * SLOT
        low = pl.multiple_of(slot + y_hi * ROWS, ROWS)
        high = pl.multiple_of(slot + (1 - y_hi) * ROWS, ROWS)
        both[pl.ds(low, ROWS)] = near[order * ROWS : (order + 1) * ROWS]
        both[pl.ds(high, ROWS)] = twin[order * ROWS : (order + 1) * ROWS]
    part = contract(tok[...], both[...], 1, 0)
    if not first:
        part = part + sums[...]
    out[...] = (part * SCALE).astype(BF) if last else part
    masked = live_rows(cotangent[...], at)
    grad[...] = (contract(masked, both[...], 1, 1) * SCALE).astype(BF)


def use_weight(tokens, cotangent, pair, state, at, step, last):
    count = tokens.shape[0]
    first = state is None
    width = NZ * SLOT
    wide = pl.BlockSpec((count, width), lambda i, at: (0, lax.rem(at[0] + step, NX)))
    block = whole(NZ * ROWS, KV)
    ins = [(tokens, wide), (cotangent, whole(count, KV)), (pair[0], block), (pair[1], block)]
    aliases = None
    if not first:
        ins += [(state[0], whole(count, KV)), (state[1], pl.BlockSpec(memory_space=pl.ANY))]
        aliases = {len(ins): 1}
    outs = [((count, KV), BF if last else F32, whole(count, KV)), ((count, D), BF, wide)]
    kernel = functools.partial(weight_kernel, first, last)
    flops = 4 * count * KV * width
    return call(kernel, (1,), at, ins, outs, flops, 6 << 20, [pltpu.VMEM((width, KV), BF)], aliases)


def exchange(tokens, cotangent, local_w, at):
    rows, send = first_block(tokens, cotangent, at)
    rows_q = rows[PART:]
    local_w, send = together(local_w, send)
    twin_1 = moved(send, dy=2)
    low, high = [moved(local_w, dz=1)], [moved(local_w, dz=-1)]
    low[0], high[0], twin_1 = together(low[0], high[0], twin_1)

    low.append(moved(low[0], dz=1))
    high.append(moved(high[0], dz=-1))
    send = twin_blocks(tokens, rows_q, at, (3, -3))
    right, left = far_block(tokens, rows, twin_1, at)
    low[1], high[1], right, left, send = together(low[1], high[1], right, left, send)

    right, left = moved(right, dz=1), moved(left, dz=-1)
    low.append(moved(low[1], dz=1))
    high.append(moved(high[1], dz=-1))
    twin_2 = moved(send, dy=2)
    send = twin_blocks(tokens, rows_q, at, (2, -2))
    low[2], high[2], send = together(low[2], high[2], send)
    half = ROWS // 2
    far = moved(low[2][:half], dz=1), moved(high[2][half:], dz=-1)

    right = step_block(tokens, rows, twin_2, 0, right, at, 3)
    right, left = together(right, left)
    left = step_block(tokens, rows, twin_2, 1, left, at, -3)
    right, left, send, *far = together(right, left, send, *far)
    right, left = moved(right, dz=1), moved(left, dz=-1)
    twin_3 = moved(send, dy=2)
    near = jnp.concatenate([local_w] + high + list(far) + low[::-1], axis=0)
    send = twin_blocks(tokens, rows_q, at, (1, -1, 0))
    near, send = together(near, send)
    near_low, near_high = moved(near, dx=1), moved(near, dx=-1)
    twin = moved(near, dy=2)
    twin_4 = moved(send, dy=2)

    right = step_block(tokens, rows, twin_3, 0, right, at, 2)
    right, left = together(right, left)
    left = step_block(tokens, rows, twin_3, 1, left, at, -2)
    right, left = together(right, left)
    right, left = moved(right, dz=1), moved(left, dz=-1)
    near_low, near_high, twin = together(near_low, near_high, twin)
    twin_low, twin_high = moved(twin, dx=1), moved(twin, dx=-1)
    state = use_weight(tokens, cotangent, (near, twin), None, at, 0, False)

    right = step_block(tokens, rows, twin_4, 0, right, at, 1)
    right, left = together(right, left)
    left = step_block(tokens, rows, twin_4, 1, left, at, -1)
    right, left, *state = together(right, left, *state)
    right, left = moved(right, dz=1), moved(left, dz=-1)
    twin_low, twin_high = together(twin_low, twin_high)
    near_far, twin_far = moved(near_low, dx=1), moved(twin_high, dx=-1)
    state = use_weight(tokens, cotangent, (near_high, twin_high), state, at, 1, False)
    state = use_weight(tokens, cotangent, (near_low, twin_low), state, at, 3, False)
    right, left, *state = together(right, left, *state)

    own, *pieces = last_block(tokens, rows, twin_4, 2, right, left, at)
    came = spread_x(pieces)
    keep, send = split_y(own, came, at)
    came = moved(send, dy=2)
    state = use_weight(tokens, cotangent, (near_far, twin_far), state, at, 2, True)
    return state, (keep, came)


def update_kernel(
    frag, keep, came, weight, moment, second, anchor, velocity, two, far,
    weight_out, moment_out, second_out, anchor_out, velocity_out, drift_out, stepped,
):
    low = keep[:PART] + came[...].astype(F32)
    grad = jnp.concatenate([low, keep[PART:]], axis=0).T * SCALE
    first = 0.9 * moment[0].astype(F32) + 0.1 * grad
    sec = 0.95 * second[0].astype(F32) + 0.05 * grad * grad
    old = weight[0].astype(F32)
    value = old - 0.01 * (first / (jnp.sqrt(sec) + 1e-08) + 0.1 * old)
    moment_out[0] = first.astype(BF)
    second_out[0] = sec.astype(BF)
    weight_out[0] = value.astype(BF)
    stepped[...] = value

    def columns(order):
        return pl.ds(pl.multiple_of(frag[order] * HEAD, HEAD), HEAD)

    for order in range(KV // HEAD):
        cols = columns(order)
        drift_out[0, :, order * HEAD : (order + 1) * HEAD] = anchor[:, cols] - stepped[:, cols]
    cols = columns(0)
    mean = two[0].astype(F32) + two[1].astype(F32) + far[0].astype(F32) + far[1].astype(F32)
    mean = mean * 0.25
    velocity_new = 0.9 * velocity[:, cols] + mean
    anchor_new = anchor[:, cols] - 0.7 * (mean + 0.9 * velocity_new)
    velocity_out[...] = velocity_new
    anchor_out[...] = anchor_new
    weight_out[0, :, cols] = (0.5 * stepped[:, cols] + 0.5 * anchor_new).astype(BF)


def update(fragment, parts, weight, moment, second, anchor, velocity, two, far):
    values = (*parts, weight, moment, second, anchor, velocity, two, far)
    ins = [(value, whole(*value.shape)) for value in values]
    wide, narrow = (1, ROWS, KV), (ROWS, HEAD)
    kinds = [(wide, BF), (wide, BF), (wide, BF), (narrow, F32), (narrow, F32), (wide, F32)]
    outs = [(shape, kind, whole(*shape)) for shape, kind in kinds]
    scratch = [pltpu.VMEM((ROWS, KV), F32)]
    return call(update_kernel, (1,), fragment, ins, outs, 2 << 20, 3 << 20, scratch)


def per_device(
    tokens, weight, moment, second, cotangent, lengths, fragment, anchor, velocity, outer_grad
):
    place = lax.axis_index("fsdp")
    x, z, y_hi = place // (NZ * NY), (place // NY) % NZ, place % NY
    local_x, local_c = tokens[0], cotangent[0]
    tok_count = local_x.shape[0]

    seq_count = lengths.shape[1]
    holders = NX * NZ * NY // seq_count
    limit = lax.dynamic_index_in_dim(lengths[0], place // holders, keepdims=False)
    live = limit - (place % holders) * tok_count
    at = jnp.stack([x, z, y_hi, live]).astype(jnp.int32)

    (projected, input_grad), parts = exchange(local_x, local_c, weight[0], at)

    outer_own = outer_grad[0]
    outer_two = jnp.stack([outer_own, moved(outer_own, dcore=1)])
    outer_far = swap_y_lo(outer_two)

    weight_new, moment_new, second_new, anchor_new, velocity_new, drift = update(
        fragment, parts, weight, moment, second, anchor, velocity, outer_two, outer_far
    )
    return (
        projected[None],
        input_grad[None],
        weight_new,
        moment_new,
        second_new,
        anchor_new,
        velocity_new,
        drift,
    )


def solution(mesh):
    wide = P("rep", "fsdp", None)
    return jax.shard_map(
        per_device,
        mesh=mesh,
        in_specs=(
            wide,
            wide,
            wide,
            wide,
            wide,
            P("rep", None),
            P(),
            P("fsdp", None),
            P("fsdp", None),
            wide,
        ),
        out_specs=(
            wide,
            wide,
            wide,
            wide,
            wide,
            P("fsdp", None),
            P("fsdp", None),
            wide,
        ),
        check_vma=False,
    )
```

```python
import functools
import math

import jax
import jax.numpy as jnp
from jax import lax
from jax.experimental import pallas as pl
from jax.experimental.pallas import tpu as pltpu
from jax.sharding import PartitionSpec as P

D = 8192
KV = 512
HEAD = 128
NX, NZ, NY = 4, 8, 2
SLOT = D // (NX * NZ)
ROWS = SLOT // NY
PART = KV // 2
LOAD = 3 * D // (2 * NZ)
SCALE = 1.0 / math.sqrt(D)
AXES = ("rep", "fsdp")
BF = jnp.bfloat16
F32 = jnp.float32


def device_index(x, z, y, core):
    y_hi, y_lo = y // 2, y % 2
    return (y_lo * 2 + core) * 64 + (x * NZ + z) * NY + y_hi


def moved(value, dx=0, dz=0, dy=0, dcore=0):
    pairs = []
    for x in range(NX):
        for z in range(NZ):
            for y in range(4):
                for core in range(2):
                    source = device_index(x, z, y, core)
                    target = device_index(
                        (x + dx) % NX, (z + dz) % NZ, (y + dy) % 4, (core + dcore) % 2
                    )
                    pairs.append((source, target))
    return lax.ppermute(value, AXES, sorted(pairs))


def swap_y_lo(value):
    pairs = []
    for rep in range(4):
        for place in range(64):
            pairs.append((rep * 64 + place, (rep ^ 2) * 64 + place))
    return lax.ppermute(value, AXES, pairs)


def together(*values):
    return lax.optimization_barrier(values)


def both_ways(to_right, to_left, axis):
    to_right, to_left = together(to_right, to_left)
    return together(moved(to_right, **{axis: 1}), moved(to_left, **{axis: -1}))


def contract(left, right, left_dim, right_dim):
    return lax.dot_general(
        left, right, (((left_dim,), (right_dim,)), ((), ())), preferred_element_type=F32
    )


def call(
    kernel, grid, scalars, ins, outs, flops, moved_bytes, scratch=(), aliases=None, limit=20
):
    shapes = [jax.ShapeDtypeStruct(shape, kind) for shape, kind, _ in outs]
    return pl.pallas_call(
        kernel,
        out_shape=shapes,
        grid_spec=pltpu.PrefetchScalarGridSpec(
            num_scalar_prefetch=1,
            grid=grid,
            in_specs=[spec for _, spec in ins],
            out_specs=[spec for _, _, spec in outs],
            scratch_shapes=list(scratch),
        ),
        input_output_aliases=aliases or {},
        compiler_params=pltpu.CompilerParams(vmem_limit_bytes=limit << 20),
        cost_estimate=pl.CostEstimate(
            flops=flops, bytes_accessed=moved_bytes, transcendentals=0
        ),
    )(scalars, *[value for value, _ in ins])


def whole(*shape):
    return pl.BlockSpec(shape, lambda *_: (0,) * len(shape))


def live_rows(cotangent, at):
    row = lax.broadcasted_iota(jnp.int32, cotangent.shape, 0)
    return jnp.where(row < at[3], cotangent, jnp.zeros_like(cotangent))


def token_specs(count, shift, y=None):
    def spec(col):
        if y is None:
            return pl.BlockSpec((count, SLOT), lambda i, at: (0, col * NZ + lax.rem(at[1] + shift, NZ)))

        def place(i, at):
            z = lax.rem(at[1] + (shift(i) if callable(shift) else shift), NZ)
            return 0, (col * NZ + z) * NY + (at[2] if y == 0 else 1 - at[2])

        return pl.BlockSpec((count, ROWS), place)

    return [spec(col) for col in range(NX)]


def joined(refs):
    return jnp.concatenate([ref[...] for ref in refs], axis=1)


def first_kernel(at, *refs):
    toks, (cotangent, rows, out) = refs[:NX], refs[NX:]
    rows[...] = live_rows(cotangent[...], at).T
    out[0] = contract(rows[PART:], joined(toks), 1, 0).astype(BF)


def first_block(tokens, cotangent, at):
    count = tokens.shape[0]
    ins = [(tokens, spec) for spec in token_specs(count, lambda i: NZ // 2, 1)]
    ins += [(cotangent, whole(count, KV))]
    outs = [((KV, count), BF, whole(KV, count))]
    outs += [((1, PART, NX * ROWS), BF, whole(1, PART, NX * ROWS))]
    return call(first_kernel, (1,), at, ins, outs, PART * count * NX * SLOT, 1 << 20)


def twin_kernel(at, *refs):
    toks, rows, out = refs[:NX], *refs[NX:]
    out[0] = contract(rows[...], joined(toks), 1, 0).astype(BF)


def twin_blocks(tokens, rows, at, steps):
    count = tokens.shape[0]

    def shift(i):
        value = steps[-1] % NZ
        for order in range(len(steps) - 2, -1, -1):
            value = jnp.where(i == order, steps[order] % NZ, value)
        return value

    ins = [(tokens, spec) for spec in token_specs(count, shift, 1)] + [(rows, whole(PART, count))]
    block = pl.BlockSpec((1, PART, NX * ROWS), lambda i, at: (i, 0, 0))
    outs = [((len(steps), PART, NX * ROWS), BF, block)]
    flops = 2 * PART * count * NX * ROWS * len(steps)
    return call(twin_kernel, (len(steps),), at, ins, outs, flops, len(steps) << 19)[0]


def terms(toks, rows, y_hi):
    wide = [contract(rows[:PART], tok[...], 1, 0) for tok in toks]
    begin = pl.multiple_of(y_hi * ROWS, ROWS)
    narrow = jnp.concatenate([tok[:, pl.ds(begin, ROWS)] for tok in toks], axis=1)
    return wide + [contract(rows[PART:], narrow, 1, 0)]


def far_kernel(at, *refs):
    toks, (rows, came, out_r, out_l) = refs[:NX], refs[NX:]
    parts = terms(toks, rows, at[2])
    parts[NX] = parts[NX] + came[0].astype(F32)
    value = jnp.concatenate(parts, axis=1).astype(BF)
    out_r[...] = value[: PART // 2]
    out_l[...] = value[PART // 2 :]


def far_block(tokens, rows, came, at):
    count = tokens.shape[0]
    ins = [(tokens, spec) for spec in token_specs(count, 4)]
    ins += [(rows, whole(KV, count)), (came, whole(1, PART, NX * ROWS))]
    outs = [((PART // 2, LOAD), BF, whole(PART // 2, LOAD))] * 2
    return call(far_kernel, (1,), at, ins, outs, 2 * PART * count * LOAD, 3 << 19)


def step_kernel(upper, at, *refs):
    toks, (rows, came, moving, out) = refs[:NX], refs[NX:]
    parts = terms(toks, rows, at[2])
    parts[NX] = parts[NX] + came[0].astype(F32)
    size = moving.shape[0]
    begin = PART - size if upper else 0
    col = 0
    for part in parts:
        cols = slice(col, col + part.shape[1])
        col += part.shape[1]
        rows_in = slice(begin, begin + size)
        out[rows_in, cols] = (part[rows_in] + moving[:, cols].astype(F32)).astype(BF)
        if size < PART:
            rest = slice(0, begin) if upper else slice(size, PART)
            out[rest, cols] = part[rest].astype(BF)


def step_block(tokens, rows, came, order, moving, at, step):
    count = tokens.shape[0]
    ins = [(tokens, spec) for spec in token_specs(count, step % NZ)]
    ins += [
        (rows, whole(KV, count)),
        (came, pl.BlockSpec((1, PART, NX * ROWS), lambda i, at: (order, 0, 0))),
        (moving, whole(*moving.shape)),
    ]
    outs = [((PART, LOAD), BF, whole(PART, LOAD))]
    kernel = functools.partial(step_kernel, step < 0)
    return call(kernel, (1,), at, ins, outs, 2 * PART * count * LOAD, 5 << 19)[0]


def last_kernel(at, tok, rows, came, *refs):
    moving_p, moving_q, (own, out_1, out_2, out_3) = refs[:2], refs[2:4], refs[4:]
    i = pl.program_id(0)
    wide, narrow = terms([tok], rows, at[2])
    wide = wide + (moving_p[0][...].astype(F32) + moving_p[1][...].astype(F32))
    narrow = narrow + came[0].astype(F32)
    narrow = narrow + (moving_q[0][...].astype(F32) + moving_q[1][...].astype(F32))
    for step, out in ((0, own), (1, out_1), (2, out_2), (3, out_3)):

        @pl.when(i == step)
        def _(out=out):
            out[:, :SLOT] = wide.astype(out.dtype)
            out[:, SLOT:] = narrow.astype(out.dtype)


def last_block(tokens, rows, came, order, right, left, at):
    count = tokens.shape[0]

    def column(i, at):
        return lax.rem(at[0] + i, NX)

    tok = pl.BlockSpec((count, SLOT), lambda i, at: (0, column(i, at) * NZ + at[1]))
    wide = pl.BlockSpec((PART, SLOT), lambda i, at: (0, column(i, at)))
    narrow = pl.BlockSpec((PART, ROWS), lambda i, at: (0, NX * NY + column(i, at)))
    twin = pl.BlockSpec((1, PART, ROWS), lambda i, at: (order, 0, column(i, at)))
    ins = [(tokens, tok), (rows, whole(KV, count)), (came, twin)]
    ins += [(right, wide), (left, wide), (right, narrow), (left, narrow)]
    size = SLOT + ROWS
    outs = [((PART, size), F32, whole(PART, size))]
    outs += [((PART, size), BF, whole(PART, size))] * 3
    return call(last_kernel, (NX,), at, ins, outs, 2 * PART * count * LOAD, 4 << 20)


def split_kernel(at, own, in_1, in_2, in_3, keep, send):
    value = own[...] + (
        in_1[...].astype(F32) + in_2[...].astype(F32) + in_3[...].astype(F32)
    )
    keep[PART:] = value[:, SLOT:]
    for y in range(NY):

        @pl.when(at[2] == y)
        def _(y=y):
            keep[:PART] = value[:, y * ROWS : (y + 1) * ROWS]
            send[...] = value[:, (1 - y) * ROWS : (2 - y) * ROWS].astype(BF)


def split_y(own, came, at):
    full = whole(PART, SLOT + ROWS)
    ins = [(own, full)] + [(value, full) for value in came]
    outs = [((KV, ROWS), F32, whole(KV, ROWS)), ((PART, ROWS), BF, whole(PART, ROWS))]
    return call(split_kernel, (1,), at, ins, outs, 1 << 20, 3 << 19)


def spread_x(pieces):
    pieces = together(*pieces)
    return together(*[moved(value, dx=step) for step, value in zip((1, 2, 3), pieces)])


def weight_kernel(first, last, at, tok, cotangent, near, twin, *rest):
    sums, (out, grad, both) = (None if first else rest[0]), rest[-3:]
    z, y_hi = at[1], at[2]
    for order in range(NZ):
        slot = lax.rem(z + order, NZ) * SLOT
        low = pl.multiple_of(slot + y_hi * ROWS, ROWS)
        high = pl.multiple_of(slot + (1 - y_hi) * ROWS, ROWS)
        both[pl.ds(low, ROWS)] = near[order * ROWS : (order + 1) * ROWS]
        both[pl.ds(high, ROWS)] = twin[order * ROWS : (order + 1) * ROWS]
    part = contract(tok[...], both[...], 1, 0)
    if not first:
        part = part + sums[...]
    out[...] = (part * SCALE).astype(BF) if last else part
    masked = live_rows(cotangent[...], at)
    grad[...] = (contract(masked, both[...], 1, 1) * SCALE).astype(BF)


def use_weight(tokens, cotangent, pair, state, at, step, last):
    count = tokens.shape[0]
    first = state is None
    width = NZ * SLOT
    wide = pl.BlockSpec((count, width), lambda i, at: (0, lax.rem(at[0] + step, NX)))
    block = whole(NZ * ROWS, KV)
    ins = [(tokens, wide), (cotangent, whole(count, KV)), (pair[0], block), (pair[1], block)]
    aliases = None
    if not first:
        ins += [(state[0], whole(count, KV)), (state[1], pl.BlockSpec(memory_space=pl.ANY))]
        aliases = {len(ins): 1}
    outs = [((count, KV), BF if last else F32, whole(count, KV)), ((count, D), BF, wide)]
    kernel = functools.partial(weight_kernel, first, last)
    flops = 4 * count * KV * width
    return call(kernel, (1,), at, ins, outs, flops, 6 << 20, [pltpu.VMEM((width, KV), BF)], aliases)


def exchange(tokens, cotangent, local_w, at):
    rows, send = first_block(tokens, cotangent, at)
    rows_q = rows[PART:]
    local_w, send = together(local_w, send)
    twin_1 = moved(send, dy=2)
    low, high = [moved(local_w, dz=1)], [moved(local_w, dz=-1)]
    low[0], high[0], twin_1 = together(low[0], high[0], twin_1)

    low.append(moved(low[0], dz=1))
    high.append(moved(high[0], dz=-1))
    send = twin_blocks(tokens, rows_q, at, (3, -3))
    right, left = far_block(tokens, rows, twin_1, at)
    low[1], high[1], right, left, send = together(low[1], high[1], right, left, send)

    right, left = moved(right, dz=1), moved(left, dz=-1)
    low.append(moved(low[1], dz=1))
    high.append(moved(high[1], dz=-1))
    twin_2 = moved(send, dy=2)
    send = twin_blocks(tokens, rows_q, at, (2, -2))
    low[2], high[2], send = together(low[2], high[2], send)
    half = ROWS // 2
    far = moved(low[2][:half], dz=1), moved(high[2][half:], dz=-1)

    right = step_block(tokens, rows, twin_2, 0, right, at, 3)
    right, left = together(right, left)
    left = step_block(tokens, rows, twin_2, 1, left, at, -3)
    right, left, send, *far = together(right, left, send, *far)
    right, left = moved(right, dz=1), moved(left, dz=-1)
    twin_3 = moved(send, dy=2)
    near = jnp.concatenate([local_w] + high + list(far) + low[::-1], axis=0)
    send = twin_blocks(tokens, rows_q, at, (1, -1, 0))
    near, send = together(near, send)
    near_low, near_high = moved(near, dx=1), moved(near, dx=-1)
    twin = moved(near, dy=2)
    twin_4 = moved(send, dy=2)

    right = step_block(tokens, rows, twin_3, 0, right, at, 2)
    right, left = together(right, left)
    left = step_block(tokens, rows, twin_3, 1, left, at, -2)
    right, left = together(right, left)
    right, left = moved(right, dz=1), moved(left, dz=-1)
    near_low, near_high, twin = together(near_low, near_high, twin)
    twin_low, twin_high = moved(twin, dx=1), moved(twin, dx=-1)
    state = use_weight(tokens, cotangent, (near, twin), None, at, 0, False)

    right = step_block(tokens, rows, twin_4, 0, right, at, 1)
    right, left = together(right, left)
    left = step_block(tokens, rows, twin_4, 1, left, at, -1)
    right, left, *state = together(right, left, *state)
    right, left = moved(right, dz=1), moved(left, dz=-1)
    twin_low, twin_high = together(twin_low, twin_high)
    near_far, twin_far = moved(near_low, dx=1), moved(twin_high, dx=-1)
    state = use_weight(tokens, cotangent, (near_high, twin_high), state, at, 1, False)
    state = use_weight(tokens, cotangent, (near_low, twin_low), state, at, 3, False)
    right, left, *state = together(right, left, *state)

    own, *pieces = last_block(tokens, rows, twin_4, 2, right, left, at)
    came = spread_x(pieces)
    keep, send = split_y(own, came, at)
    keep, send, *state = together(keep, send, *state)
    came = moved(send, dy=2)
    state = use_weight(tokens, cotangent, (near_far, twin_far), state, at, 2, True)
    keep, came, state = together(keep, came, state)
    return state, (keep, came)


def update_kernel(
    frag, keep, came, weight, moment, second, anchor, velocity, two, far,
    weight_out, moment_out, second_out, anchor_out, velocity_out, drift_out, stepped,
):
    low = keep[:PART] + came[...].astype(F32)
    grad = jnp.concatenate([low, keep[PART:]], axis=0).T * SCALE
    first = 0.9 * moment[0].astype(F32) + 0.1 * grad
    sec = 0.95 * second[0].astype(F32) + 0.05 * grad * grad
    old = weight[0].astype(F32)
    value = old - 0.01 * (first / (jnp.sqrt(sec) + 1e-08) + 0.1 * old)
    moment_out[0] = first.astype(BF)
    second_out[0] = sec.astype(BF)
    weight_out[0] = value.astype(BF)
    stepped[...] = value

    def columns(order):
        return pl.ds(pl.multiple_of(frag[order] * HEAD, HEAD), HEAD)

    for order in range(KV // HEAD):
        cols = columns(order)
        drift_out[0, :, order * HEAD : (order + 1) * HEAD] = anchor[:, cols] - stepped[:, cols]
    cols = columns(0)
    mean = two[0].astype(F32) + two[1].astype(F32) + far[0].astype(F32) + far[1].astype(F32)
    mean = mean * 0.25
    velocity_new = 0.9 * velocity[:, cols] + mean
    anchor_new = anchor[:, cols] - 0.7 * (mean + 0.9 * velocity_new)
    velocity_out[...] = velocity_new
    anchor_out[...] = anchor_new
    weight_out[0, :, cols] = (0.5 * stepped[:, cols] + 0.5 * anchor_new).astype(BF)


def update(fragment, parts, weight, moment, second, anchor, velocity, two, far):
    values = (*parts, weight, moment, second, anchor, velocity, two, far)
    ins = [(value, whole(*value.shape)) for value in values]
    wide, narrow = (1, ROWS, KV), (ROWS, HEAD)
    kinds = [(wide, BF), (wide, BF), (wide, BF), (narrow, F32), (narrow, F32), (wide, F32)]
    outs = [(shape, kind, whole(*shape)) for shape, kind in kinds]
    scratch = [pltpu.VMEM((ROWS, KV), F32)]
    return call(update_kernel, (1,), fragment, ins, outs, 2 << 20, 3 << 20, scratch)


def per_device(
    tokens, weight, moment, second, cotangent, lengths, fragment, anchor, velocity, outer_grad
):
    place = lax.axis_index("fsdp")
    x, z, y_hi = place // (NZ * NY), (place // NY) % NZ, place % NY
    local_x, local_c = tokens[0], cotangent[0]
    tok_count = local_x.shape[0]

    seq_count = lengths.shape[1]
    holders = NX * NZ * NY // seq_count
    limit = lax.dynamic_index_in_dim(lengths[0], place // holders, keepdims=False)
    live = limit - (place % holders) * tok_count
    at = jnp.stack([x, z, y_hi, live]).astype(jnp.int32)

    (projected, input_grad), parts = exchange(local_x, local_c, weight[0], at)

    outer_own = outer_grad[0]
    outer_two = jnp.stack([outer_own, moved(outer_own, dcore=1)])
    outer_far = swap_y_lo(outer_two)

    weight_new, moment_new, second_new, anchor_new, velocity_new, drift = update(
        fragment, parts, weight, moment, second, anchor, velocity, outer_two, outer_far
    )
    return (
        projected[None],
        input_grad[None],
        weight_new,
        moment_new,
        second_new,
        anchor_new,
        velocity_new,
        drift,
    )


def solution(mesh):
    wide = P("rep", "fsdp", None)
    return jax.shard_map(
        per_device,
        mesh=mesh,
        in_specs=(
            wide,
            wide,
            wide,
            wide,
            wide,
            P("rep", None),
            P(),
            P("fsdp", None),
            P("fsdp", None),
            wide,
        ),
        out_specs=(
            wide,
            wide,
            wide,
            wide,
            wide,
            P("fsdp", None),
            P("fsdp", None),
            wide,
        ),
        check_vma=False,
    )
```
